128 devices in a mesh: ctx: 16 (over x, y_lo, core), mp: 8 (over y_hi, z).
Axes of the slice: x: 4, y: 4 (y_hi: 2, y_lo: 2; y = y_hi * 2 + y_lo), z: 4, core: 2. Of those that a mesh axis runs over, the one named last changes fastest.
Arguments:
- prompt_queries: bfloat16 [8192, 8192], P('ctx', 'mp'), may hold values from -21 to 21
- prompt_keys: bfloat16 [8192, 1024], P('ctx', 'mp'), may hold values from -21 to 21
- prompt_values: bfloat16 [8192, 1024], P('ctx', 'mp'), may hold values from -6 to 6
- step_queries: bfloat16 [2, 32, 8192], P(None, 'ctx', 'mp'), may hold values from -21 to 21
- step_keys: bfloat16 [2, 32, 1024], P(None, 'ctx', 'mp'), may hold values from -10 to 10
- step_values: bfloat16 [2, 32, 1024], P(None, 'ctx', 'mp'), may hold values from -6 to 6
- block_owners: int32 [64], P('ctx'), may hold values from 0 to 7, as said below
- prompt_lengths: int32 [4], replicated, may hold values from 512 to 5120, as said below
- row_request: int32 [32], replicated, may hold values from 0 to 3
Outputs:
- prefill_output: bfloat16 [8192, 8192], P('ctx', 'mp')
- owned_keys: bfloat16 [16, 8, 2, 128, 1024], P('ctx', 'mp')
- owned_values: bfloat16 [16, 8, 2, 128, 1024], P('ctx', 'mp')
- decode_output: bfloat16 [2, 32, 8192], P(None, 'ctx', 'mp')
The draws below stay inside these ranges and needn't reach their ends.
Inputs may be any that keep to these rules, and one draw needn't show every extreme that they name: `block_owners`: among the 4 blocks of one index of ctx, no owner receives more than 2, and in every draw one owner receives exactly 2 blocks from every index of ctx. `prompt_lengths`: the 4 prompts lie end to end; their lengths sum to 8192; exactly one prompt has 5120 tokens.
All inputs are finite; a program needn't handle non-finite values.
Results may differ from the reference program's by a relative error of at most 0.02.
Values may be sent and summed in bfloat16 or wider, within the bound.
A program may use at most 832 MiB of HBM per device.

```python
import functools
import math
import jax
import jax.numpy as jnp
from jax import lax

H = 64
KVH = 8
HD = 128
REQS = 4
BT = 128
STEPS = 2
SEQ = 8192
ROWS = 32
BLK_DEV = 4
CAP = 2
LMIN = 512
N_CTX = 16
N_MP = 8


def prompt_split(key):
    key = jax.random.fold_in(key, 11)
    hot_key, weight_key = jax.random.split(key)
    favoured = jax.random.randint(hot_key, (), 0, REQS)
    indices = jnp.arange(REQS, dtype=jnp.int32)
    weights = jax.random.randint(weight_key, (REQS,), 1, 9)
    weights = jnp.where(indices == favoured, 0, weights)
    spare_tokens = SEQ - REQS * LMIN
    major_spare = spare_tokens * 3 // 4
    rest_spare = spare_tokens - major_spare
    extra_tokens = rest_spare * weights // jnp.sum(weights)
    leftover = rest_spare - jnp.sum(extra_tokens)
    extra_tokens = extra_tokens + jnp.where(indices == (favoured + 1) % REQS, leftover, 0)
    extra_tokens = extra_tokens + jnp.where(indices == favoured, major_spare, 0)
    return (LMIN + extra_tokens).astype(jnp.int32)


def draw_prompt_lengths(key, part):
    return prompt_split(key)


def draw_prompt_keys(key, part):
    key = jax.random.fold_in(key, 3)
    base_draw = jnp.clip(jax.random.normal(key, (SEQ, KVH * HD), jnp.float32), -4.0, 4.0)
    return base_draw.astype(jnp.bfloat16)


def draw_prompt_queries(key, part):
    key = jax.random.fold_in(key, 4)
    base_draw = jnp.clip(jax.random.normal(key, (SEQ, H * HD), jnp.float32), -4.0, 4.0)
    return base_draw.astype(jnp.bfloat16)


def draw_step_queries(key, part):
    key = jax.random.fold_in(key, 6)
    base_draw = jnp.clip(jax.random.normal(key, (STEPS, ROWS, H * HD), jnp.float32), -4.0, 4.0)
    return base_draw.astype(jnp.bfloat16)


def shuffled(sub_key):
    return jax.random.permutation(sub_key, BLK_DEV)


def draw_block_owners(key, part):
    key = jax.random.fold_in(key, 5)
    hot_key, order_key, other_key = jax.random.split(key, 3)
    favoured = jax.random.randint(hot_key, (), 0, N_MP)
    ranking = jax.vmap(shuffled)(jax.random.split(order_key, N_CTX))
    others = jax.random.randint(other_key, (N_CTX, BLK_DEV), 0, N_MP - 1)
    others = others + (others >= favoured).astype(jnp.int32)
    owners = jnp.where(ranking < CAP, favoured, others)
    return owners.reshape(N_CTX * BLK_DEV).astype(jnp.int32)


def plant(values, stream_key, least, top_value):
    longest = values.shape.index(max(values.shape))
    spots = []
    for shift in (0, 1):
        where = [jax.random.randint(jax.random.fold_in(stream_key, axis), (), 0, length) for axis, length in enumerate(values.shape)]
        where[longest] = (where[longest] + shift) % values.shape[longest]
        spots.append(tuple(where))
    return values.at[spots[0]].set(least).at[spots[1]].set(top_value)


def steps_of(stream_key, shape, pieces, low, largest):
    factor_of, own = 1.0, jax.random.fold_in(stream_key, 6)
    for position, blocks in pieces:
        steps = jnp.exp(jax.random.uniform(jax.random.fold_in(own, position), (blocks,), jnp.float32, low / len(pieces), largest / len(pieces)))
        factor_of = factor_of * jnp.repeat(steps, shape[position] // blocks).reshape([-1 if axis == position else 1 for axis in range(len(shape))])
    return factor_of


def centred(rng, extent, spread, limit, shards=(), kind=jnp.bfloat16):
    factor_of = steps_of(rng, extent, shards, -0.22, 0.18) if shards else 1.0
    values = jax.random.normal(rng, extent, jnp.float32) * spread * factor_of
    return jnp.minimum(jnp.maximum(values, -limit), limit).astype(kind)


def setup_inputs(seed: int = 0) -> dict:
    key_of = jax.random.split(jax.random.key(seed), 10)
    return {
        "prompt_queries": draw_prompt_queries(jax.random.fold_in(key_of[9], 71), 0),
        "prompt_keys": draw_prompt_keys(jax.random.fold_in(key_of[9], 71), 0),
        "prompt_values": centred(key_of[2], (SEQ, KVH * HD), 1.0, 6.0, ((0, 16), (1, 8))),
        "step_queries": draw_step_queries(jax.random.fold_in(key_of[9], 71), 0),
        "step_keys": centred(key_of[4], (STEPS, ROWS, KVH * HD), 2.5, 10.0, ((1, 16), (2, 8))),
        "step_values": centred(key_of[5], (STEPS, ROWS, KVH * HD), 1.0, 6.0, ((1, 16), (2, 8))),
        "block_owners": draw_block_owners(jax.random.fold_in(key_of[9], 71), 0),
        "prompt_lengths": draw_prompt_lengths(jax.random.fold_in(key_of[9], 71), 0),
        "row_request": plant(jax.random.randint(key_of[8], (ROWS,), 0, REQS), jax.random.fold_in(key_of[8], 1), 0, REQS - 1).astype(jnp.int32),
    }


NEG_FILL = -1e+30

def request_of(positions, prompt_lengths):
    endings = jnp.cumsum(prompt_lengths).astype(jnp.int32)
    return lax.optimization_barrier(jnp.sum((positions[:, None] >= endings[None, :]).astype(jnp.int32), axis=1))

def to_bf16(tensor):
    return lax.optimization_barrier(tensor.astype(jnp.bfloat16)).astype(jnp.float32)

def slot_table(owners_run, owner_count):
    block_count = owners_run.shape[0]
    indices = jnp.arange(block_count, dtype=jnp.int32)
    earlier = (owners_run[:, None] == owners_run[None, :]) & (indices[None, :] < indices[:, None])
    slot_index = lax.optimization_barrier(jnp.sum(earlier.astype(jnp.int32), axis=1))
    target = owners_run * CAP + slot_index
    slot_ids = jnp.arange(owner_count * CAP, dtype=jnp.int32)
    return (target[None, :] == slot_ids[:, None]).astype(jnp.int32)

def prefill(prompt_queries, prompt_keys, prompt_values, prompt_lengths):
    seq_len = prompt_queries.shape[0]
    group_size = H // KVH
    score_scale = 1.0 / math.sqrt(HD)
    positions = jnp.arange(seq_len, dtype=jnp.int32)
    request = request_of(positions, prompt_lengths)
    block_rows = math.gcd(seq_len, 1024)
    outputs = []
    for row_begin in range(0, seq_len, block_rows):
        row_end = row_begin + block_rows
        query_part = prompt_queries[row_begin:row_end].astype(jnp.float32).reshape(block_rows, KVH, group_size, HD)
        key_part = prompt_keys[:row_end].astype(jnp.float32).reshape(row_end, KVH, HD)
        value_part = prompt_values[:row_end].astype(jnp.float32).reshape(row_end, KVH, HD)
        allowed = (positions[row_begin:row_end, None] >= positions[None, :row_end]) & (request[row_begin:row_end, None] == request[None, :row_end])

        def one_head(operands, allowed=allowed):
            query_head, key_head, value_head = operands
            scores = jnp.einsum('qgd,kd->gqk', query_head, key_head) * score_scale
            scores = jnp.where(allowed[None], scores, NEG_FILL)
            highest = lax.optimization_barrier(jnp.max(scores, axis=2, keepdims=True))
            weights = jnp.where(allowed[None], jnp.exp(scores - highest), 0.0)
            totals = lax.optimization_barrier(jnp.sum(weights, axis=2))
            running = jnp.einsum('gqk,kd->gqd', to_bf16(weights), value_head)
            return running / totals[..., None]
        heads_out = lax.map(one_head, (jnp.moveaxis(query_part, 1, 0), jnp.moveaxis(key_part, 1, 0), jnp.moveaxis(value_part, 1, 0)))
        outputs.append(jnp.transpose(heads_out, (2, 0, 1, 3)).reshape(block_rows, H * HD).astype(jnp.bfloat16))
    return jnp.concatenate(outputs, axis=0)

def pages(prompt_cache, block_owners):
    runs = block_owners.reshape(N_CTX, BLK_DEV)
    tables = jax.vmap(functools.partial(slot_table, owner_count=N_MP))(runs)
    block_data = prompt_cache.reshape(N_CTX, BLK_DEV, BT, KVH * HD).astype(jnp.float32)
    picked = jnp.einsum('cob,cbtd->cotd', tables.astype(jnp.float32), block_data)
    return picked.reshape(N_CTX, N_MP, CAP, BT, KVH * HD).astype(jnp.bfloat16)

def decode(step_queries, step_keys, step_values, prompt_keys, prompt_values, prompt_lengths, row_request):
    seq_len = prompt_keys.shape[0]
    row_total = step_queries.shape[1]
    group_size = H // KVH
    score_scale = 1.0 / math.sqrt(HD)
    request = request_of(jnp.arange(seq_len, dtype=jnp.int32), prompt_lengths)
    visible = (row_request[:, None] == request[None, :])[None, :, None, :]
    step_ids = jnp.arange(STEPS, dtype=jnp.int32)
    earlier = (step_ids[None, :] <= step_ids[:, None])[:, None, None, :]
    query_all = step_queries.astype(jnp.float32).reshape(STEPS, row_total, KVH, group_size, HD)
    fresh_keys = step_keys.astype(jnp.float32).reshape(STEPS, row_total, KVH, HD)
    fresh_values = step_values.astype(jnp.float32).reshape(STEPS, row_total, KVH, HD)
    cache_keys = prompt_keys.astype(jnp.float32).reshape(seq_len, KVH, HD)
    cache_values = prompt_values.astype(jnp.float32).reshape(seq_len, KVH, HD)

    def one_head(operands):
        query_head, key_fresh, value_fresh, key_cache, value_cache = operands
        prompt_scores = jnp.einsum('srgd,kd->srgk', query_head, key_cache) * score_scale
        prompt_scores = jnp.where(visible, prompt_scores, NEG_FILL)
        own_scores = jnp.einsum('srgd,urd->srgu', query_head, key_fresh) * score_scale
        own_scores = jnp.where(earlier, own_scores, NEG_FILL)
        highest = jnp.maximum(lax.optimization_barrier(jnp.max(prompt_scores, axis=-1)), lax.optimization_barrier(jnp.max(own_scores, axis=-1)))[..., None]
        prompt_weights = jnp.where(visible, jnp.exp(prompt_scores - highest), 0.0)
        own_weights = jnp.where(earlier, jnp.exp(own_scores - highest), 0.0)
        totals = lax.optimization_barrier(jnp.sum(prompt_weights, axis=-1)) + lax.optimization_barrier(jnp.sum(own_weights, axis=-1))
        running = jnp.einsum('srgk,kd->srgd', to_bf16(prompt_weights), value_cache)
        running = running + jnp.einsum('srgu,urd->srgd', to_bf16(own_weights), value_fresh)
        return running / totals[..., None]
    heads_out = lax.map(one_head, (jnp.moveaxis(query_all, 2, 0), jnp.moveaxis(fresh_keys, 2, 0), jnp.moveaxis(fresh_values, 2, 0), jnp.moveaxis(cache_keys, 1, 0), jnp.moveaxis(cache_values, 1, 0)))
    return jnp.transpose(heads_out, (1, 2, 0, 3, 4)).reshape(STEPS, row_total, H * HD).astype(jnp.bfloat16)

def reference(prompt_queries, prompt_keys, prompt_values, step_queries, step_keys, step_values, block_owners, prompt_lengths, row_request):
    prefill_output = prefill(prompt_queries, prompt_keys, prompt_values, prompt_lengths)
    owned_keys = pages(prompt_keys, block_owners)
    owned_values = pages(prompt_values, block_owners)
    decode_output = decode(step_queries, step_keys, step_values, prompt_keys, prompt_values, prompt_lengths, row_request)
    return (prefill_output, owned_keys, owned_values, decode_output)
```

```python
import functools
import math

import jax
import jax.numpy as jnp
from jax import lax
from jax.experimental import pallas as pl
from jax.experimental.pallas import tpu as pltpu
from jax.sharding import PartitionSpec as P

HEADS = 8
HD = 128
ROWS = 512
HALF = 256
BT = 128
NBLK = 16
SEQ = NBLK * ROWS
STEP_ROWS = 128
REACH = 10
NEG = -1e30
C = math.log2(math.e) / math.sqrt(HD)
F32 = jnp.float32
BF16 = jnp.bfloat16
MESH = pl.DeviceIdType.MESH
N_MP = 8


def score(queries, keys):
    return lax.dot_general(queries, keys, (((1,), (1,)), ((), ())), preferred_element_type=F32)


def kernel(
    lengths, row_request, owners,
    q_ref, k_ref, v_ref, sq_ref, sk_ref, sv_ref,
    out_ref, dec_ref, pk_ref, pv_ref,
    kv, mk, mq, acc, tot, high, s0, s1, n0, n1, f0, f1, qd, sd, tail, pages_k, pages_v,
    send_sem, recv_sem, psend_sem, precv_sem, self_sem,
):
    ctx = lax.axis_index("ctx")
    mp = lax.axis_index("mp")
    x, y, core = ctx // 4, (ctx // 2) % 2, ctx % 2

    def place(xx, yy, kk):
        return ((xx + 4) % 4) * 4 + yy * 2 + kk

    sib = place(x, y, 1 - core)
    across = place(x, 1 - y, core)
    right = place(x + 1, y, core)
    left = place(x - 1, y, core)

    barrier = pltpu.get_barrier_semaphore()
    for other in (sib, across, right, left):
        pl.semaphore_signal(barrier, inc=1, device_id=(other, mp), device_id_type=MESH)
    for d in range(1, N_MP):
        pl.semaphore_signal(
            barrier, inc=1, device_id=(ctx, (mp + d) % N_MP), device_id_type=MESH
        )

    def rows_of(block):
        return pl.ds(pl.multiple_of(block * ROWS, ROWS), ROWS)

    own = rows_of(ctx)
    kv[own, :HD] = k_ref[...]
    kv[own, HD:] = v_ref[...]
    pl.semaphore_wait(barrier, 4 + N_MP - 1)

    def send(block, to, slot):
        return pltpu.make_async_remote_copy(
            src_ref=kv.at[rows_of(block)],
            dst_ref=kv.at[rows_of(block)],
            send_sem=send_sem.at[slot],
            recv_sem=recv_sem.at[block],
            device_id=(to, mp),
            device_id_type=MESH,
        )

    def arrived(block):
        send(block, sib, 0).wait_recv()

    sent = []

    def forward(block, targets):
        for to in targets:
            copy = send(block, to, len(sent))
            copy.start()
            sent.append(copy)

    forward(ctx, (across, right, left, sib))

    lane = lax.broadcasted_iota(jnp.int32, (1, HD), 1)
    e0 = lengths[0]
    e1 = e0 + lengths[1]
    e2 = e1 + lengths[2]
    begin = jnp.where(lane == 1, e0, jnp.where(lane == 2, e1, jnp.where(lane == 3, e2, 0)))
    end = jnp.where(
        lane == 0, e0, jnp.where(lane == 1, e1, jnp.where(lane == 2, e2, jnp.where(lane == 3, SEQ, 0)))
    )

    def belongs(first, count):
        pos = first + lax.broadcasted_iota(jnp.int32, (count, HD), 0)
        return (pos >= begin) & (pos < end)

    def fill(block, _):
        mk[rows_of(block), :] = jnp.where(belongs(block * ROWS, ROWS), 1.0, 0.0).astype(BF16)
        return 0

    lax.fori_loop(0, NBLK, fill, 0)
    wide = lax.broadcasted_iota(jnp.int32, (ROWS, HD), 1)
    mq[...] = jnp.where(belongs(ctx * ROWS, ROWS) | (wide >= 4), 0.0, NEG).astype(BF16)

    own_of = [owners[b] for b in range(4)]
    slot_of = []
    for b in range(4):
        earlier = jnp.int32(0)
        for a in range(b):
            earlier = earlier + jnp.where(own_of[a] == own_of[b], 1, 0)
        slot_of.append(earlier)

    def fill_page(t, _):
        o, s = t // 2, t % 2
        picked_k = jnp.zeros((BT, HD), F32)
        picked_v = jnp.zeros((BT, HD), F32)
        for b in range(4):
            hit = jnp.where((own_of[b] == o) & (slot_of[b] == s), 1.0, 0.0).astype(F32)
            picked_k = picked_k + hit * k_ref[b * BT : (b + 1) * BT, :].astype(F32)
            picked_v = picked_v + hit * v_ref[b * BT : (b + 1) * BT, :].astype(F32)
        pages_k[o, s] = picked_k.astype(BF16)
        pages_v[o, s] = picked_v.astype(BF16)
        return 0

    lax.fori_loop(0, 2 * N_MP, fill_page, 0)
    mine = pl.ds(pl.multiple_of(mp * HD, HD), HD)
    paged = []
    for d in range(1, N_MP):
        to = (mp + d) % N_MP
        for i, (source, target) in enumerate(((pages_k, pk_ref), (pages_v, pv_ref))):
            copy = pltpu.make_async_remote_copy(
                src_ref=source.at[to],
                dst_ref=target.at[:, :, mine],
                send_sem=psend_sem.at[i, d],
                recv_sem=precv_sem.at[i, d],
                device_id=(ctx, to),
                device_id_type=MESH,
            )
            copy.start()
            paged.append(copy)
    kept = []
    for i, (source, target) in enumerate(((pages_k, pk_ref), (pages_v, pv_ref))):
        copy = pltpu.make_async_copy(source.at[mp], target.at[:, :, mine], self_sem.at[i])
        copy.start()
        kept.append(copy)

    def tile_of(h, half):
        return pl.ds(pl.multiple_of(h * ROWS + half * HALF, HALF), HALF)

    def produce(h, half, blocks, columns, s_ref, n_ref, f_ref, diagonal):
        rows = pl.ds(half * HALF, HALF)
        queries = jnp.concatenate(
            [q_ref[rows, pl.ds(pl.multiple_of(h * HD, HD), HD)], mq[rows, :]], axis=1
        )
        best = None
        for i, block in enumerate(blocks):
            span = pl.ds(pl.multiple_of(block * ROWS, ROWS), columns)
            s = score(queries, jnp.concatenate([kv[span, :HD], mk[span, :]], axis=1))
            if diagonal:
                at = lax.broadcasted_iota(jnp.int32, s.shape, 0) + half * HALF
                s = jnp.where(at >= lax.broadcasted_iota(jnp.int32, s.shape, 1), s, NEG)
            s_ref[:, i * columns : (i + 1) * columns] = s
            for j in range(0, columns, HD):
                part = s[:, j : j + HD]
                best = part if best is None else jnp.maximum(best, part)
        best = jnp.max(best, axis=1, keepdims=True)
        if diagonal:
            n_ref[...] = jnp.broadcast_to(best, (HALF, HD))
        else:
            before = high[tile_of(h, half), :]
            now = jnp.maximum(before, best)
            n_ref[...] = now
            f_ref[...] = jnp.exp2((before - now) * C)

    def consume(h, half, blocks, columns, s_ref, n_ref, f_ref, diagonal):
        at = tile_of(h, half)
        now = n_ref[...]
        total = None
        running = None
        for i, block in enumerate(blocks):
            span = pl.ds(pl.multiple_of(block * ROWS, ROWS), columns)
            parts = []
            for j in range(i * columns, (i + 1) * columns, HD):
                weight = jnp.exp2((s_ref[:, j : j + HD] - now) * C)
                total = weight if total is None else total + weight
                parts.append(weight.astype(BF16))
            product = jnp.dot(
                jnp.concatenate(parts, axis=1), kv[span, HD:], preferred_element_type=F32
            )
            running = product if running is None else running + product
        high[at, :] = now
        if diagonal:
            acc[at, :] = running
            tot[at, :] = total
        else:
            fade = f_ref[...]
            acc[at, :] = acc[at, :] * fade + running
            tot[at, :] = tot[at, :] * fade + total

    def attend(blocks, diagonal=False):
        def stage(work, h, half):
            columns = HALF if diagonal and half == 0 else ROWS
            slot = (s1, n1, f1) if half else (s0, n0, f0)
            work(h, half, blocks, columns, *slot, diagonal)

        stage(produce, 0, 0)

        def body(h, _):
            stage(produce, h, 1)
            stage(consume, h, 0)
            stage(produce, h + 1, 0)
            stage(consume, h, 1)
            return 0

        lax.fori_loop(0, HEADS - 1, body, 0)
        stage(produce, HEADS - 1, 1)
        stage(consume, HEADS - 1, 0)
        stage(consume, HEADS - 1, 1)

    attend((ctx,), diagonal=True)

    chip = ctx // 2

    def nth(n):
        rank = (n - core + 2) // 2 - 1
        near = rank + 1
        swapped = jnp.minimum(rank + 2 - 2 * ((rank + 2) % 2), 5)
        before = jnp.where(y == 1, near, swapped)
        inside = 1 - (n - core + 2) % 2
        return jnp.where((n == 0) & (core == 1), sib, (chip - before) * 2 + inside)

    count = jnp.minimum(ctx, REACH)

    def spot(dx, dy, other_core):
        return place(x + dx, (y + dy) % 2, (core + other_core) % 2)

    def event(dx, dy, targets):
        block = spot(dx, dy, 0)
        arrived(block)
        forward(block, targets + (sib,))

    def mirrored(dx, dy):
        arrived(spot(dx, dy, 1))

    def events(step):
        if step == 0:
            mirrored(0, 0)
            event(0, 1, (right, left))
            event(-1, 0, (right,))
            event(1, 0, ())
            mirrored(0, 1)
            mirrored(-1, 0)
            mirrored(1, 0)
        if step == 1:
            event(1, 1, (left,))
            event(-1, 1, ())
            mirrored(1, 1)
            mirrored(-1, 1)
        if step == 2:
            event(2, 0, ())
            mirrored(2, 0)
        if step == 3:
            event(2, 1, ())
            mirrored(2, 1)

    for step in range(REACH // 2):
        events(step)

        @pl.when(2 * step + 1 < count)
        def _(step=step):
            attend((nth(2 * step), nth(2 * step + 1)))

    @pl.when(count % 2 == 1)
    def _():
        attend((nth(count - 1),))

    def finish(h, _):
        at = pl.ds(pl.multiple_of(h * ROWS, ROWS), ROWS)
        total = jnp.sum(tot[at, :], axis=1, keepdims=True)
        out_ref[:, pl.ds(pl.multiple_of(h * HD, HD), HD)] = (acc[at, :] / total).astype(BF16)
        return 0

    lax.fori_loop(0, HEADS, finish, 0)

    for h in range(HEADS):
        for t in range(2):
            qd[h * 4 + t * 2 : h * 4 + t * 2 + 2, :HD] = sq_ref[
                t, :, h * HD : (h + 1) * HD
            ].astype(F32)
    drow = lax.broadcasted_iota(jnp.int32, (4 * HEADS, HD), 0)
    dlane = lax.broadcasted_iota(jnp.int32, (4 * HEADS, HD), 1)
    drow_t, drow_r = (drow & 3) >> 1, drow & 1
    asked = jnp.where(drow_r == 0, row_request[ctx * 2], row_request[ctx * 2 + 1])
    key_u, key_r = ((dlane - 4) & 3) >> 1, (dlane - 4) & 1
    allowed = ((dlane < 4) & (dlane == asked)) | (
        (dlane >= 4) & (dlane < 8) & (key_r == drow_r) & (key_u <= drow_t)
    )
    qd[:, HD:] = jnp.where(allowed | (dlane > 8), 0.0, NEG)
    queries = qd[...].astype(BF16)
    tail[...] = jnp.zeros_like(tail)
    for t in range(2):
        tail[t * 2 : t * 2 + 2, :HD] = sk_ref[t].astype(F32)
        tail[t * 2 : t * 2 + 2, HD:] = sv_ref[t].astype(F32)
    trow = lax.broadcasted_iota(jnp.int32, (STEP_ROWS, HD), 0)
    tlane = lax.broadcasted_iota(jnp.int32, (STEP_ROWS, HD), 1)
    tmask = jnp.where(tlane == jnp.where(trow < 4, trow + 4, 8), 1.0, 0.0).astype(BF16)
    s = score(queries, jnp.concatenate([tail[:, :HD].astype(BF16), tmask], axis=1))
    sd[:, SEQ:] = s
    best = s
    chunk = 1024
    for k in range(0, SEQ, chunk):
        s = score(queries, jnp.concatenate([kv[k : k + chunk, :HD], mk[k : k + chunk, :]], axis=1))
        sd[:, k : k + chunk] = s
        for j in range(0, chunk, HD):
            best = jnp.maximum(best, s[:, j : j + HD])
    best = jnp.max(best, axis=1, keepdims=True)
    weight = jnp.exp2((sd[:, SEQ:] - best) * C)
    total = weight
    running = jnp.dot(weight.astype(BF16), tail[:, HD:].astype(BF16), preferred_element_type=F32)
    for k in range(0, SEQ, chunk):
        parts = []
        for j in range(k, k + chunk, HD):
            weight = jnp.exp2((sd[:, j : j + HD] - best) * C)
            total = total + weight
            parts.append(weight.astype(BF16))
        running = running + jnp.dot(
            jnp.concatenate(parts, axis=1), kv[k : k + chunk, HD:], preferred_element_type=F32
        )
    result = running / jnp.sum(total, axis=1, keepdims=True)
    for h in range(HEADS):
        for t in range(2):
            dec_ref[t, :, h * HD : (h + 1) * HD] = result[
                h * 4 + t * 2 : h * 4 + t * 2 + 2, :
            ].astype(BF16)

    for copy in sent:
        copy.wait_send()
    for copy in kept:
        copy.wait()
    for copy in paged:
        copy.wait()


def on_device(q, k, v, sq, sk, sv, owners, lengths, row_request):
    vmem = pl.BlockSpec(memory_space=pltpu.VMEM)
    smem = pl.BlockSpec(memory_space=pltpu.SMEM)
    hbm = pl.BlockSpec(memory_space=pl.ANY)
    out, dec, pk, pv = pl.pallas_call(
        kernel,
        out_shape=(
            jax.ShapeDtypeStruct((ROWS, HEADS * HD), BF16),
            jax.ShapeDtypeStruct(sq.shape, BF16),
            jax.ShapeDtypeStruct((2, BT, N_MP * HD), BF16),
            jax.ShapeDtypeStruct((2, BT, N_MP * HD), BF16),
        ),
        in_specs=[smem] * 3 + [vmem] * 6,
        out_specs=(vmem, vmem, hbm, hbm),
        scratch_shapes=[
            pltpu.VMEM((SEQ, 2 * HD), BF16),
            pltpu.VMEM((SEQ, HD), BF16),
            pltpu.VMEM((ROWS, HD), BF16),
            pltpu.VMEM((HEADS * ROWS, HD), F32),
            pltpu.VMEM((HEADS * ROWS, HD), F32),
            pltpu.VMEM((HEADS * ROWS, HD), F32),
            pltpu.VMEM((HALF, 2 * ROWS), F32),
            pltpu.VMEM((HALF, 2 * ROWS), F32),
            pltpu.VMEM((HALF, HD), F32),
            pltpu.VMEM((HALF, HD), F32),
            pltpu.VMEM((HALF, HD), F32),
            pltpu.VMEM((HALF, HD), F32),
            pltpu.VMEM((4 * HEADS, 2 * HD), F32),
            pltpu.VMEM((4 * HEADS, SEQ + STEP_ROWS), F32),
            pltpu.VMEM((STEP_ROWS, 2 * HD), F32),
            pltpu.VMEM((N_MP, 2, BT, HD), BF16),
            pltpu.VMEM((N_MP, 2, BT, HD), BF16),
            pltpu.SemaphoreType.DMA((NBLK,)),
            pltpu.SemaphoreType.DMA((NBLK,)),
            pltpu.SemaphoreType.DMA((2, N_MP)),
            pltpu.SemaphoreType.DMA((2, N_MP)),
            pltpu.SemaphoreType.DMA((2,)),
        ],
        compiler_params=pltpu.CompilerParams(
            collective_id=0, has_side_effects=True, vmem_limit_bytes=56 * 2**20
        ),
        name="prefill_decode",
    )(lengths, row_request, owners, q, k, v, sq, sk, sv)
    shape = (1, 1, 2, BT, N_MP * HD)
    return out, pk.reshape(shape), pv.reshape(shape), dec


def solution(mesh):
    split = P("ctx", "mp")
    steps = P(None, "ctx", "mp")
    paged = P("ctx", "mp", None, None, None)
    return jax.shard_map(
        on_device,
        mesh=mesh,
        in_specs=(split, split, split, steps, steps, steps, P("ctx"), P(), P()),
        out_specs=(split, paged, paged, steps),
        check_vma=False,
    )
```

```python
import functools
import math

import jax
import jax.numpy as jnp
from jax import lax
from jax.experimental import pallas as pl
from jax.experimental.pallas import tpu as pltpu
from jax.sharding import PartitionSpec as P

HEADS = 8
HD = 128
ROWS = 512
HALF = ROWS // 2
BT = 128
NBLK = 16
SEQ = NBLK * ROWS
STEP_ROWS = 128
REACH = 10
NEG = -1e30
C = math.log2(math.e) / math.sqrt(HD)
F32 = jnp.float32
BF16 = jnp.bfloat16
MESH = pl.DeviceIdType.MESH
N_MP = 8


def score(queries, keys):
    return lax.dot_general(queries, keys, (((1,), (1,)), ((), ())), preferred_element_type=F32)


def kernel(
    lengths, row_request, owners,
    q_ref, k_ref, v_ref, sq_ref, sk_ref, sv_ref,
    out_ref, dec_ref, pk_ref, pv_ref,
    kv, mk, mq, acc, tot, high, s0, s1, n0, n1, f0, f1, qd, sd, tail, pages_k, pages_v,
    send_sem, recv_sem, psend_sem, precv_sem, self_sem,
):
    ctx = lax.axis_index("ctx")
    mp = lax.axis_index("mp")
    x, y, core = ctx // 4, (ctx // 2) % 2, ctx % 2

    def place(xx, yy, kk):
        return ((xx + 4) % 4) * 4 + yy * 2 + kk

    sib = place(x, y, 1 - core)
    across = place(x, 1 - y, core)
    right = place(x + 1, y, core)
    left = place(x - 1, y, core)

    barrier = pltpu.get_barrier_semaphore()
    for other in (sib, across, right, left):
        pl.semaphore_signal(barrier, inc=1, device_id=(other, mp), device_id_type=MESH)
    for d in range(1, N_MP):
        pl.semaphore_signal(
            barrier, inc=1, device_id=(ctx, (mp + d) % N_MP), device_id_type=MESH
        )

    def rows_of(block):
        return pl.ds(pl.multiple_of(block * ROWS, ROWS), ROWS)

    own = rows_of(ctx)
    kv[own, :HD] = k_ref[...]
    kv[own, HD:] = v_ref[...]
    pl.semaphore_wait(barrier, 4 + N_MP - 1)

    def send(block, to, slot):
        return pltpu.make_async_remote_copy(
            src_ref=kv.at[rows_of(block)],
            dst_ref=kv.at[rows_of(block)],
            send_sem=send_sem.at[slot],
            recv_sem=recv_sem.at[block],
            device_id=(to, mp),
            device_id_type=MESH,
        )

    def arrived(block):
        send(block, sib, 0).wait_recv()

    sent = []

    def forward(block, targets):
        for to in targets:
            copy = send(block, to, len(sent))
            copy.start()
            sent.append(copy)

    forward(ctx, (across, right, left, sib))

    lane = lax.broadcasted_iota(jnp.int32, (1, HD), 1)
    e0 = lengths[0]
    e1 = e0 + lengths[1]
    e2 = e1 + lengths[2]
    begin = jnp.where(lane == 1, e0, jnp.where(lane == 2, e1, jnp.where(lane == 3, e2, 0)))
    end = jnp.where(
        lane == 0, e0, jnp.where(lane == 1, e1, jnp.where(lane == 2, e2, jnp.where(lane == 3, SEQ, 0)))
    )

    def belongs(first, count):
        pos = first + lax.broadcasted_iota(jnp.int32, (count, HD), 0)
        return (pos >= begin) & (pos < end)

    def fill(block, _):
        mk[rows_of(block), :] = jnp.where(belongs(block * ROWS, ROWS), 1.0, 0.0).astype(BF16)
        return 0

    lax.fori_loop(0, NBLK, fill, 0)
    wide = lax.broadcasted_iota(jnp.int32, (ROWS, HD), 1)
    mq[...] = jnp.where(belongs(ctx * ROWS, ROWS) | (wide >= 4), 0.0, NEG).astype(BF16)

    own_of = [owners[b] for b in range(4)]
    slot_of = []
    for b in range(4):
        earlier = jnp.int32(0)
        for a in range(b):
            earlier = earlier + jnp.where(own_of[a] == own_of[b], 1, 0)
        slot_of.append(earlier)

    def fill_page(t, _):
        o, s = t // 2, t % 2
        picked_k = jnp.zeros((BT, HD), F32)
        picked_v = jnp.zeros((BT, HD), F32)
        for b in range(4):
            hit = jnp.where((own_of[b] == o) & (slot_of[b] == s), 1.0, 0.0).astype(F32)
            picked_k = picked_k + hit * k_ref[b * BT : (b + 1) * BT, :].astype(F32)
            picked_v = picked_v + hit * v_ref[b * BT : (b + 1) * BT, :].astype(F32)
        pages_k[o, s] = picked_k.astype(BF16)
        pages_v[o, s] = picked_v.astype(BF16)
        return 0

    lax.fori_loop(0, 2 * N_MP, fill_page, 0)
    mine = pl.ds(pl.multiple_of(mp * HD, HD), HD)
    paged = []
    for d in range(1, N_MP):
        to = (mp + d) % N_MP
        for i, (source, target) in enumerate(((pages_k, pk_ref), (pages_v, pv_ref))):
            copy = pltpu.make_async_remote_copy(
                src_ref=source.at[to],
                dst_ref=target.at[:, :, mine],
                send_sem=psend_sem.at[i, d],
                recv_sem=precv_sem.at[i, d],
                device_id=(ctx, to),
                device_id_type=MESH,
            )
            copy.start()
            paged.append(copy)
    kept = []
    for i, (source, target) in enumerate(((pages_k, pk_ref), (pages_v, pv_ref))):
        copy = pltpu.make_async_copy(source.at[mp], target.at[:, :, mine], self_sem.at[i])
        copy.start()
        kept.append(copy)

    def tile_of(h, first=0, count=ROWS):
        return pl.ds(pl.multiple_of(h * ROWS + first, HALF), count)

    def bands(diagonal):
        return ((0, HALF, HALF), (HALF, HALF, ROWS)) if diagonal else ((0, ROWS, ROWS),)

    def produce(h, blocks, s_ref, n_ref, f_ref, diagonal, fresh):
        for first, count, columns in bands(diagonal):
            rows = pl.ds(first, count)
            queries = jnp.concatenate(
                [q_ref[rows, pl.ds(pl.multiple_of(h * HD, HD), HD)], mq[rows, :]], axis=1
            )
            best = None
            for i, block in enumerate(blocks):
                span = pl.ds(pl.multiple_of(block * ROWS, ROWS), columns)
                s = score(queries, jnp.concatenate([kv[span, :HD], mk[span, :]], axis=1))
                if diagonal:
                    at = lax.broadcasted_iota(jnp.int32, s.shape, 0) + first
                    s = jnp.where(at >= lax.broadcasted_iota(jnp.int32, s.shape, 1), s, NEG)
                s_ref[rows, i * columns : (i + 1) * columns] = s
                for j in range(0, columns, HD):
                    part = s[:, j : j + HD]
                    best = part if best is None else jnp.maximum(best, part)
            best = jnp.max(best, axis=1, keepdims=True)
            if fresh:
                n_ref[rows, :] = jnp.broadcast_to(best, (count, HD))
            else:
                before = high[tile_of(h, first, count), :]
                now = jnp.maximum(before, best)
                n_ref[rows, :] = now
                f_ref[rows, :] = jnp.exp2((before - now) * C)

    def consume(h, blocks, s_ref, n_ref, f_ref, diagonal, fresh):
        for first, count, columns in bands(diagonal):
            rows = pl.ds(first, count)
            at = tile_of(h, first, count)
            now = n_ref[rows, :]
            total = None
            running = None
            for i, block in enumerate(blocks):
                span = pl.ds(pl.multiple_of(block * ROWS, ROWS), columns)
                parts = []
                for j in range(i * columns, (i + 1) * columns, HD):
                    weight = jnp.exp2((s_ref[rows, j : j + HD] - now) * C)
                    total = weight if total is None else total + weight
                    parts.append(weight.astype(BF16))
                product = jnp.dot(
                    jnp.concatenate(parts, axis=1), kv[span, HD:], preferred_element_type=F32
                )
                running = product if running is None else running + product
            high[at, :] = now
            if fresh:
                acc[at, :] = running
                tot[at, :] = total
            else:
                fade = f_ref[rows, :]
                acc[at, :] = acc[at, :] * fade + running
                tot[at, :] = tot[at, :] * fade + total

    def stage(work, h, odd, blocks, diagonal=False, fresh=False):
        slot = (s1, n1, f1) if odd else (s0, n0, f0)
        work(h, blocks, *slot, diagonal, fresh)

    def attend(blocks, diagonal=False, fresh=False):
        kind = (blocks, diagonal, fresh)
        stage(produce, 0, 0, *kind)

        def body(i, _):
            stage(produce, 2 * i + 1, 1, *kind)
            stage(consume, 2 * i, 0, *kind)
            stage(produce, 2 * i + 2, 0, *kind)
            stage(consume, 2 * i + 1, 1, *kind)
            return 0

        lax.fori_loop(0, HEADS // 2 - 1, body, 0)
        stage(produce, HEADS - 1, 1, *kind)
        stage(consume, HEADS - 2, 0, *kind)
        stage(consume, HEADS - 1, 1, *kind)

    attend((ctx,), diagonal=True, fresh=True)

    chip = ctx // 2

    def nth(n):
        rank = (n - core + 2) // 2 - 1
        near = rank + 1
        swapped = jnp.minimum(rank + 2 - 2 * ((rank + 2) % 2), 5)
        before = jnp.where(y == 1, near, swapped)
        inside = 1 - (n - core + 2) % 2
        return jnp.where((n == 0) & (core == 1), sib, (chip - before) * 2 + inside)

    count = jnp.minimum(ctx, REACH)

    def spot(dx, dy, other_core):
        return place(x + dx, (y + dy) % 2, (core + other_core) % 2)

    def event(dx, dy, targets):
        block = spot(dx, dy, 0)
        arrived(block)
        forward(block, targets + (sib,))

    def mirrored(dx, dy):
        arrived(spot(dx, dy, 1))

    def events(step):
        if step == 0:
            mirrored(0, 0)
            event(0, 1, (right, left))
            event(-1, 0, (right,))
            event(1, 0, ())
            mirrored(0, 1)
            mirrored(-1, 0)
            mirrored(1, 0)
        if step == 1:
            event(1, 1, (left,))
            event(-1, 1, ())
            mirrored(1, 1)
            mirrored(-1, 1)
        if step == 2:
            event(2, 0, ())
            mirrored(2, 0)
        if step == 3:
            event(2, 1, ())
            mirrored(2, 1)

    def one_step(step, _):
        for at in range(4):

            @pl.when(step == at)
            def _(at=at):
                events(at)

        @pl.when(2 * step + 1 < count)
        def _():
            attend((nth(2 * step), nth(2 * step + 1)))

        return 0

    lax.fori_loop(0, REACH // 2, one_step, 0)

    @pl.when(count % 2 == 1)
    def _():
        attend((nth(count - 1),))

    def finished(h):
        at = pl.ds(pl.multiple_of(h * ROWS, ROWS), ROWS)
        total = jnp.sum(tot[at, :], axis=1, keepdims=True)
        return (acc[at, :] / total).astype(BF16)

    def finish(h, _):
        out_ref[:, pl.ds(pl.multiple_of(h * HD, HD), HD)] = finished(h)
        return 0

    lax.fori_loop(0, HEADS, finish, 0)

    for h in range(HEADS):
        for t in range(2):
            qd[h * 4 + t * 2 : h * 4 + t * 2 + 2, :HD] = sq_ref[
                t, :, h * HD : (h + 1) * HD
            ].astype(F32)
    drow = lax.broadcasted_iota(jnp.int32, (4 * HEADS, HD), 0)
    dlane = lax.broadcasted_iota(jnp.int32, (4 * HEADS, HD), 1)
    drow_t, drow_r = (drow & 3) >> 1, drow & 1
    asked = jnp.where(drow_r == 0, row_request[ctx * 2], row_request[ctx * 2 + 1])
    key_u, key_r = ((dlane - 4) & 3) >> 1, (dlane - 4) & 1
    allowed = ((dlane < 4) & (dlane == asked)) | (
        (dlane >= 4) & (dlane < 8) & (key_r == drow_r) & (key_u <= drow_t)
    )
    qd[:, HD:] = jnp.where(allowed | (dlane > 8), 0.0, NEG)
    queries = qd[...].astype(BF16)
    tail[...] = jnp.zeros_like(tail)
    for t in range(2):
        tail[t * 2 : t * 2 + 2, :HD] = sk_ref[t].astype(F32)
        tail[t * 2 : t * 2 + 2, HD:] = sv_ref[t].astype(F32)
    trow = lax.broadcasted_iota(jnp.int32, (STEP_ROWS, HD), 0)
    tlane = lax.broadcasted_iota(jnp.int32, (STEP_ROWS, HD), 1)
    tmask = jnp.where(tlane == jnp.where(trow < 4, trow + 4, 8), 1.0, 0.0).astype(BF16)
    s = score(queries, jnp.concatenate([tail[:, :HD].astype(BF16), tmask], axis=1))
    sd[:, SEQ:] = s
    best = s
    chunk = 1024
    for k in range(0, SEQ, chunk):
        s = score(queries, jnp.concatenate([kv[k : k + chunk, :HD], mk[k : k + chunk, :]], axis=1))
        sd[:, k : k + chunk] = s
        for j in range(0, chunk, HD):
            best = jnp.maximum(best, s[:, j : j + HD])
    best = jnp.max(best, axis=1, keepdims=True)
    weight = jnp.exp2((sd[:, SEQ:] - best) * C)
    total = weight
    running = jnp.dot(weight.astype(BF16), tail[:, HD:].astype(BF16), preferred_element_type=F32)
    for k in range(0, SEQ, chunk):
        parts = []
        for j in range(k, k + chunk, HD):
            weight = jnp.exp2((sd[:, j : j + HD] - best) * C)
            total = total + weight
            parts.append(weight.astype(BF16))
        running = running + jnp.dot(
            jnp.concatenate(parts, axis=1), kv[k : k + chunk, HD:], preferred_element_type=F32
        )
    result = running / jnp.sum(total, axis=1, keepdims=True)
    for h in range(HEADS):
        for t in range(2):
            dec_ref[t, :, h * HD : (h + 1) * HD] = result[
                h * 4 + t * 2 : h * 4 + t * 2 + 2, :
            ].astype(BF16)

    for slot in range(len(sent)):
        send(ctx, sib, slot).wait_send()
    for copy in kept:
        copy.wait()
    for copy in paged:
        copy.wait()


def copy_kernel(out, pk, pv, dec, out_to, pk_to, pv_to, dec_to, *scratch):
    held, (sem_in, sem_out) = scratch[:-2], scratch[-2:]
    parts = []
    for a, via, b in zip((out, pk, pv, dec), held, (out_to, pk_to, pv_to, dec_to)):
        for i in range(2):
            half = a.shape[0] // 2
            span = pl.ds(i * half, half)
            n = len(parts)
            parts.append(
                (
                    pltpu.make_async_copy(a.at[span], via.at[span], sem_in.at[n]),
                    pltpu.make_async_copy(via.at[span], b.at[span], sem_out.at[n]),
                )
            )
    for inward, _ in parts:
        inward.start()
    for inward, outward in parts:
        inward.wait()
        outward.start()
    for _, outward in parts:
        outward.wait()


def on_device(q, k, v, sq, sk, sv, owners, lengths, row_request):
    vmem = pl.BlockSpec(memory_space=pltpu.VMEM)
    smem = pl.BlockSpec(memory_space=pltpu.SMEM)
    hbm = pl.BlockSpec(memory_space=pl.ANY)
    out, dec, pk, pv = pl.pallas_call(
        kernel,
        out_shape=(
            jax.ShapeDtypeStruct((ROWS, HEADS * HD), BF16),
            jax.ShapeDtypeStruct(sq.shape, BF16),
            jax.ShapeDtypeStruct((2, BT, N_MP * HD), BF16),
            jax.ShapeDtypeStruct((2, BT, N_MP * HD), BF16),
        ),
        in_specs=[smem] * 3 + [vmem] * 6,
        out_specs=(vmem, vmem, hbm, hbm),
        scratch_shapes=[
            pltpu.VMEM((SEQ, 2 * HD), BF16),
            pltpu.VMEM((SEQ, HD), BF16),
            pltpu.VMEM((ROWS, HD), BF16),
            pltpu.VMEM((HEADS * ROWS, HD), F32),
            pltpu.VMEM((HEADS * ROWS, HD), F32),
            pltpu.VMEM((HEADS * ROWS, HD), F32),
            pltpu.VMEM((ROWS, 2 * ROWS), F32),
            pltpu.VMEM((ROWS, 2 * ROWS), F32),
            pltpu.VMEM((ROWS, HD), F32),
            pltpu.VMEM((ROWS, HD), F32),
            pltpu.VMEM((ROWS, HD), F32),
            pltpu.VMEM((ROWS, HD), F32),
            pltpu.VMEM((4 * HEADS, 2 * HD), F32),
            pltpu.VMEM((4 * HEADS, SEQ + STEP_ROWS), F32),
            pltpu.VMEM((STEP_ROWS, 2 * HD), F32),
            pltpu.VMEM((N_MP, 2, BT, HD), BF16),
            pltpu.VMEM((N_MP, 2, BT, HD), BF16),
            pltpu.SemaphoreType.DMA((NBLK,)),
            pltpu.SemaphoreType.DMA((NBLK,)),
            pltpu.SemaphoreType.DMA((2, N_MP)),
            pltpu.SemaphoreType.DMA((2, N_MP)),
            pltpu.SemaphoreType.DMA((2,)),
        ],
        compiler_params=pltpu.CompilerParams(
            collective_id=0, has_side_effects=True, vmem_limit_bytes=56 * 2**20
        ),
        name="prefill_decode",
    )(lengths, row_request, owners, q, k, v, sq, sk, sv)
    results = (out, pk, pv, dec)
    out, pk, pv, dec = pl.pallas_call(
        copy_kernel,
        out_shape=tuple(jax.ShapeDtypeStruct(r.shape, r.dtype) for r in results),
        in_specs=[hbm] * 4,
        out_specs=(hbm,) * 4,
        scratch_shapes=[pltpu.VMEM(r.shape, r.dtype) for r in results]
        + [pltpu.SemaphoreType.DMA((8,))] * 2,
        name="results",
    )(*results)
    shape = (1, 1, 2, BT, N_MP * HD)
    return out, pk.reshape(shape), pv.reshape(shape), dec


def solution(mesh):
    split = P("ctx", "mp")
    steps = P(None, "ctx", "mp")
    paged = P("ctx", "mp", None, None, None)
    return jax.shard_map(
        on_device,
        mesh=mesh,
        in_specs=(split, split, split, steps, steps, steps, P("ctx"), P(), P()),
        out_specs=(split, paged, paged, steps),
        check_vma=False,
    )
```

```python
import functools
import math

import jax
import jax.numpy as jnp
from jax import lax
from jax.experimental import pallas as pl
from jax.experimental.pallas import tpu as pltpu
from jax.sharding import PartitionSpec as P

HEADS = 8
HD = 128
ROWS = 512
HALF = ROWS // 2
BT = 128
NBLK = 16
SEQ = NBLK * ROWS
STEP_ROWS = 128
REACH = 10
NEG = -1e30
C = math.log2(math.e) / math.sqrt(HD)
F32 = jnp.float32
BF16 = jnp.bfloat16
MESH = pl.DeviceIdType.MESH
N_MP = 8


def score(queries, keys):
    return lax.dot_general(queries, keys, (((1,), (1,)), ((), ())), preferred_element_type=F32)


def kernel(
    lengths, row_request, owners,
    q_hbm, k_ref, v_ref, sq_ref, sk_ref, sv_ref,
    out_hbm, dec_ref, pk_ref, pv_ref,
    q_ref, out_ref, kv, mk, mq, acc, tot, high, s0, s1, n0, n1, f0, f1, qd, sd, tail, pages_k, pages_v,
    send_sem, recv_sem, psend_sem, precv_sem, self_sem, ctx_in, mp_in,
):
    ctx = lax.axis_index("ctx")
    mp = lax.axis_index("mp")
    x, y, core = ctx // 4, (ctx // 2) % 2, ctx % 2

    def place(xx, yy, kk):
        return ((xx + 4) % 4) * 4 + yy * 2 + kk

    sib = place(x, y, 1 - core)
    across = place(x, 1 - y, core)
    right = place(x + 1, y, core)
    left = place(x - 1, y, core)

    barrier = pltpu.get_barrier_semaphore()
    for near in (place(x, 1 - y, 0), place(x + 1, y, 0), place(x - 1, y, 0)):
        pl.semaphore_signal(barrier, inc=1, device_id=(near, mp), device_id_type=MESH)
    for d in range(1, N_MP):
        pl.semaphore_signal(
            barrier,
            inc=1,
            device_id=(place(x, y, 1), (mp + d) % N_MP),
            device_id_type=MESH,
        )

    @pl.when(core == 1)
    def _():
        pl.semaphore_signal(barrier, inc=1, device_id=(sib, mp), device_id_type=MESH)

    load_q = pltpu.make_async_copy(q_hbm, q_ref, self_sem.at[2])
    load_q.start()

    def rows_of(block):
        return pl.ds(pl.multiple_of(block * ROWS, ROWS), ROWS)

    own = rows_of(ctx)
    kv[own, :HD] = k_ref[...]
    kv[own, HD:] = v_ref[...]

    def tell(semaphore):
        pl.semaphore_signal(semaphore, inc=1, device_id=(sib, mp), device_id_type=MESH)

    @pl.when(core == 0)
    def _():
        pl.semaphore_wait(barrier, 7)
        tell(ctx_in)

    @pl.when(core == 1)
    def _():
        pl.semaphore_wait(ctx_in, 1)


    def send(block, to, slot):
        return pltpu.make_async_remote_copy(
            src_ref=kv.at[rows_of(block)],
            dst_ref=kv.at[rows_of(block)],
            send_sem=send_sem.at[slot],
            recv_sem=recv_sem.at[block],
            device_id=(to, mp),
            device_id_type=MESH,
        )

    def arrived(block):
        send(block, sib, 0).wait_recv()

    sent = []

    def forward(block, targets):
        for to in targets:
            copy = send(block, to, len(sent))
            copy.start()
            sent.append(copy)

    forward(ctx, (across, right, left, sib))

    lane = lax.broadcasted_iota(jnp.int32, (1, HD), 1)
    e0 = lengths[0]
    e1 = e0 + lengths[1]
    e2 = e1 + lengths[2]
    begin = jnp.where(lane == 1, e0, jnp.where(lane == 2, e1, jnp.where(lane == 3, e2, 0)))
    end = jnp.where(
        lane == 0, e0, jnp.where(lane == 1, e1, jnp.where(lane == 2, e2, jnp.where(lane == 3, SEQ, 0)))
    )

    def belongs(first, count):
        pos = first + lax.broadcasted_iota(jnp.int32, (count, HD), 0)
        return (pos >= begin) & (pos < end)

    def fill(block, _):
        mk[rows_of(block), :] = jnp.where(belongs(block * ROWS, ROWS), 1.0, 0.0).astype(BF16)
        return 0

    lax.fori_loop(0, NBLK, fill, 0)
    wide = lax.broadcasted_iota(jnp.int32, (ROWS, HD), 1)
    mq[...] = jnp.where(belongs(ctx * ROWS, ROWS) | (wide >= 4), 0.0, NEG).astype(BF16)

    own_of = [owners[b] for b in range(4)]
    slot_of = []
    for b in range(4):
        earlier = jnp.int32(0)
        for a in range(b):
            earlier = earlier + jnp.where(own_of[a] == own_of[b], 1, 0)
        slot_of.append(earlier)

    def fill_page(t, _):
        o, s = t // 2, t % 2
        picked_k = jnp.zeros((BT, HD), F32)
        picked_v = jnp.zeros((BT, HD), F32)
        for b in range(4):
            hit = jnp.where((own_of[b] == o) & (slot_of[b] == s), 1.0, 0.0).astype(F32)
            picked_k = picked_k + hit * k_ref[b * BT : (b + 1) * BT, :].astype(F32)
            picked_v = picked_v + hit * v_ref[b * BT : (b + 1) * BT, :].astype(F32)
        pages_k[o, s] = picked_k.astype(BF16)
        pages_v[o, s] = picked_v.astype(BF16)
        return 0

    lax.fori_loop(0, 2 * N_MP, fill_page, 0)
    mine = pl.ds(pl.multiple_of(mp * HD, HD), HD)
    pages = ((pages_k, pk_ref), (pages_v, pv_ref))

    def page_copies():
        copies = []
        for d in range(1, N_MP):
            to = (mp + d) % N_MP
            for i, (source, target) in enumerate(pages):
                copies.append(
                    pltpu.make_async_remote_copy(
                        src_ref=source.at[to],
                        dst_ref=target.at[:, :, mine],
                        send_sem=psend_sem.at[i, d],
                        recv_sem=precv_sem.at[i, d],
                        device_id=(ctx, to),
                        device_id_type=MESH,
                    )
                )
        return copies

    def send_pages():
        @pl.when(core == 1)
        def _():
            pl.semaphore_wait(barrier, 2 * (N_MP - 1))
            tell(mp_in)

        @pl.when(core == 0)
        def _():
            pl.semaphore_wait(mp_in, 1)

        for copy in page_copies():
            copy.start()

    kept = []
    for i, (source, target) in enumerate(pages):
        copy = pltpu.make_async_copy(source.at[mp], target.at[:, :, mine], self_sem.at[i])
        copy.start()
        kept.append(copy)

    def tile_of(h, first=0, count=ROWS):
        return pl.ds(pl.multiple_of(h * ROWS + first, HALF), count)

    def bands(diagonal):
        return ((0, HALF, HALF), (HALF, HALF, ROWS)) if diagonal else ((0, ROWS, ROWS),)

    def produce(h, blocks, s_ref, n_ref, f_ref, diagonal, fresh):
        for first, count, columns in bands(diagonal):
            rows = pl.ds(first, count)
            queries = jnp.concatenate(
                [q_ref[rows, pl.ds(pl.multiple_of(h * HD, HD), HD)], mq[rows, :]], axis=1
            )
            best = None
            for i, block in enumerate(blocks):
                span = pl.ds(pl.multiple_of(block * ROWS, ROWS), columns)
                s = score(queries, jnp.concatenate([kv[span, :HD], mk[span, :]], axis=1))
                if diagonal:
                    at = lax.broadcasted_iota(jnp.int32, s.shape, 0) + first
                    s = jnp.where(at >= lax.broadcasted_iota(jnp.int32, s.shape, 1), s, NEG)
                s_ref[rows, i * columns : (i + 1) * columns] = s
                for j in range(0, columns, HD):
                    part = s[:, j : j + HD]
                    best = part if best is None else jnp.maximum(best, part)
            best = jnp.max(best, axis=1, keepdims=True)
            if fresh:
                n_ref[rows, :] = jnp.broadcast_to(best, (count, HD))
            else:
                before = high[tile_of(h, first, count), :]
                now = jnp.maximum(before, best)
                n_ref[rows, :] = now
                f_ref[rows, :] = jnp.exp2((before - now) * C)

    def consume(h, blocks, s_ref, n_ref, f_ref, diagonal, fresh):
        for first, count, columns in bands(diagonal):
            rows = pl.ds(first, count)
            at = tile_of(h, first, count)
            now = n_ref[rows, :]
            total = None
            running = None
            for i, block in enumerate(blocks):
                span = pl.ds(pl.multiple_of(block * ROWS, ROWS), columns)
                parts = []
                for j in range(i * columns, (i + 1) * columns, HD):
                    weight = jnp.exp2((s_ref[rows, j : j + HD] - now) * C)
                    total = weight if total is None else total + weight
                    parts.append(weight.astype(BF16))
                product = jnp.dot(
                    jnp.concatenate(parts, axis=1), kv[span, HD:], preferred_element_type=F32
                )
                running = product if running is None else running + product
            high[at, :] = now
            if fresh:
                acc[at, :] = running
                tot[at, :] = total
            else:
                fade = f_ref[rows, :]
                acc[at, :] = acc[at, :] * fade + running
                tot[at, :] = tot[at, :] * fade + total

    def stage(work, h, odd, blocks, diagonal=False, fresh=False):
        slot = (s1, n1, f1) if odd else (s0, n0, f0)
        work(h, blocks, *slot, diagonal, fresh)

    def attend(blocks, diagonal=False, fresh=False):
        kind = (blocks, diagonal, fresh)
        stage(produce, 0, 0, *kind)

        def body(i, _):
            stage(produce, 2 * i + 1, 1, *kind)
            stage(consume, 2 * i, 0, *kind)
            stage(produce, 2 * i + 2, 0, *kind)
            stage(consume, 2 * i + 1, 1, *kind)
            return 0

        lax.fori_loop(0, HEADS // 2 - 1, body, 0)
        stage(produce, HEADS - 1, 1, *kind)
        stage(consume, HEADS - 2, 0, *kind)
        stage(consume, HEADS - 1, 1, *kind)

    load_q.wait()
    attend((ctx,), diagonal=True, fresh=True)

    chip = ctx // 2

    def nth(n):
        rank = (n - core + 2) // 2 - 1
        near = rank + 1
        swapped = jnp.minimum(rank + 2 - 2 * ((rank + 2) % 2), 5)
        before = jnp.where(y == 1, near, swapped)
        inside = 1 - (n - core + 2) % 2
        return jnp.where((n == 0) & (core == 1), sib, (chip - before) * 2 + inside)

    count = jnp.minimum(ctx, REACH)

    def spot(dx, dy, other_core):
        return place(x + dx, (y + dy) % 2, (core + other_core) % 2)

    def event(dx, dy, targets):
        block = spot(dx, dy, 0)
        arrived(block)
        forward(block, targets + (sib,))

    def mirrored(dx, dy):
        arrived(spot(dx, dy, 1))

    def events(step):
        if step == 0:
            mirrored(0, 0)
            event(0, 1, (right, left))
            event(-1, 0, (right,))
            event(1, 0, ())
            mirrored(0, 1)
            mirrored(-1, 0)
            mirrored(1, 0)
        if step == 1:
            event(1, 1, (left,))
            event(-1, 1, ())
            mirrored(1, 1)
            mirrored(-1, 1)
        if step == 2:
            event(2, 0, ())
            mirrored(2, 0)
        if step == 3:
            event(2, 1, ())
            mirrored(2, 1)

    def one_step(step, _):
        for at in range(3):

            @pl.when(step == at)
            def _(at=at):
                events(at)
                if at == 0:
                    send_pages()
                if at == 2:
                    events(3)

        @pl.when((2 * step + 1 < count) & ((step < 2) | (count < REACH)))
        def _():
            attend((nth(2 * step), nth(2 * step + 1)))

        return 0

    lax.fori_loop(0, REACH // 2, one_step, 0)

    @pl.when(count == REACH)
    def _():
        attend(tuple(nth(n) for n in range(4, REACH)))

    @pl.when(count % 2 == 1)
    def _():
        attend((nth(count - 1),))

    def finished(h):
        at = pl.ds(pl.multiple_of(h * ROWS, ROWS), ROWS)
        total = jnp.sum(tot[at, :], axis=1, keepdims=True)
        return (acc[at, :] / total).astype(BF16)

    def finish(h, _):
        out_ref[:, pl.ds(pl.multiple_of(h * HD, HD), HD)] = finished(h)
        return 0

    lax.fori_loop(0, HEADS, finish, 0)
    store_out = pltpu.make_async_copy(out_ref, out_hbm, self_sem.at[3])
    store_out.start()

    for h in range(HEADS):
        for t in range(2):
            qd[h * 4 + t * 2 : h * 4 + t * 2 + 2, :HD] = sq_ref[
                t, :, h * HD : (h + 1) * HD
            ].astype(F32)
    drow = lax.broadcasted_iota(jnp.int32, (4 * HEADS, HD), 0)
    dlane = lax.broadcasted_iota(jnp.int32, (4 * HEADS, HD), 1)
    drow_t, drow_r = (drow & 3) >> 1, drow & 1
    asked = jnp.where(drow_r == 0, row_request[ctx * 2], row_request[ctx * 2 + 1])
    key_u, key_r = ((dlane - 4) & 3) >> 1, (dlane - 4) & 1
    allowed = ((dlane < 4) & (dlane == asked)) | (
        (dlane >= 4) & (dlane < 8) & (key_r == drow_r) & (key_u <= drow_t)
    )
    qd[:, HD:] = jnp.where(allowed | (dlane > 8), 0.0, NEG)
    queries = qd[...].astype(BF16)
    tail[...] = jnp.zeros_like(tail)
    for t in range(2):
        tail[t * 2 : t * 2 + 2, :HD] = sk_ref[t].astype(F32)
        tail[t * 2 : t * 2 + 2, HD:] = sv_ref[t].astype(F32)
    trow = lax.broadcasted_iota(jnp.int32, (STEP_ROWS, HD), 0)
    tlane = lax.broadcasted_iota(jnp.int32, (STEP_ROWS, HD), 1)
    tmask = jnp.where(tlane == jnp.where(trow < 4, trow + 4, 8), 1.0, 0.0).astype(BF16)
    s = score(queries, jnp.concatenate([tail[:, :HD].astype(BF16), tmask], axis=1))
    sd[:, SEQ:] = s
    best = s
    chunk = 1024
    for k in range(0, SEQ, chunk):
        s = score(queries, jnp.concatenate([kv[k : k + chunk, :HD], mk[k : k + chunk, :]], axis=1))
        sd[:, k : k + chunk] = s
        for j in range(0, chunk, HD):
            best = jnp.maximum(best, s[:, j : j + HD])
    best = jnp.max(best, axis=1, keepdims=True)
    weight = jnp.exp2((sd[:, SEQ:] - best) * C)
    total = weight
    running = jnp.dot(weight.astype(BF16), tail[:, HD:].astype(BF16), preferred_element_type=F32)
    for k in range(0, SEQ, chunk):
        parts = []
        for j in range(k, k + chunk, HD):
            weight = jnp.exp2((sd[:, j : j + HD] - best) * C)
            total = total + weight
            parts.append(weight.astype(BF16))
        running = running + jnp.dot(
            jnp.concatenate(parts, axis=1), kv[k : k + chunk, HD:], preferred_element_type=F32
        )
    result = running / jnp.sum(total, axis=1, keepdims=True)
    for h in range(HEADS):
        for t in range(2):
            dec_ref[t, :, h * HD : (h + 1) * HD] = result[
                h * 4 + t * 2 : h * 4 + t * 2 + 2, :
            ].astype(BF16)

    for slot in range(len(sent)):
        send(ctx, sib, slot).wait_send()
    for copy in kept:
        copy.wait()
    for copy in page_copies():
        copy.wait()
    store_out.wait()


def copy_kernel(out, pk, pv, dec, out_to, pk_to, pv_to, dec_to, *scratch):
    held, (sem_in, sem_out) = scratch[:-2], scratch[-2:]
    parts = []
    for a, via, b in zip((out, pk, pv, dec), held, (out_to, pk_to, pv_to, dec_to)):
        for i in range(2):
            half = a.shape[0] // 2
            span = pl.ds(i * half, half)
            n = len(parts)
            parts.append(
                (
                    pltpu.make_async_copy(a.at[span], via.at[span], sem_in.at[n]),
                    pltpu.make_async_copy(via.at[span], b.at[span], sem_out.at[n]),
                )
            )
    for inward, _ in parts:
        inward.start()
    for inward, outward in parts:
        inward.wait()
        outward.start()
    for _, outward in parts:
        outward.wait()


def on_device(q, k, v, sq, sk, sv, owners, lengths, row_request):
    vmem = pl.BlockSpec(memory_space=pltpu.VMEM)
    smem = pl.BlockSpec(memory_space=pltpu.SMEM)
    hbm = pl.BlockSpec(memory_space=pl.ANY)
    out, dec, pk, pv = pl.pallas_call(
        kernel,
        out_shape=(
            jax.ShapeDtypeStruct((ROWS, HEADS * HD), BF16),
            jax.ShapeDtypeStruct(sq.shape, BF16),
            jax.ShapeDtypeStruct((2, BT, N_MP * HD), BF16),
            jax.ShapeDtypeStruct((2, BT, N_MP * HD), BF16),
        ),
        in_specs=[smem] * 3 + [hbm] + [vmem] * 5,
        out_specs=(hbm, vmem, hbm, hbm),
        scratch_shapes=[
            pltpu.VMEM((ROWS, HEADS * HD), BF16),
            pltpu.VMEM((ROWS, HEADS * HD), BF16),
            pltpu.VMEM((SEQ, 2 * HD), BF16),
            pltpu.VMEM((SEQ, HD), BF16),
            pltpu.VMEM((ROWS, HD), BF16),
            pltpu.VMEM((HEADS * ROWS, HD), F32),
            pltpu.VMEM((HEADS * ROWS, HD), F32),
            pltpu.VMEM((HEADS * ROWS, HD), F32),
            pltpu.VMEM((ROWS, 6 * ROWS), F32),
            pltpu.VMEM((ROWS, 6 * ROWS), F32),
            pltpu.VMEM((ROWS, HD), F32),
            pltpu.VMEM((ROWS, HD), F32),
            pltpu.VMEM((ROWS, HD), F32),
            pltpu.VMEM((ROWS, HD), F32),
            pltpu.VMEM((4 * HEADS, 2 * HD), F32),
            pltpu.VMEM((4 * HEADS, SEQ + STEP_ROWS), F32),
            pltpu.VMEM((STEP_ROWS, 2 * HD), F32),
            pltpu.VMEM((N_MP, 2, BT, HD), BF16),
            pltpu.VMEM((N_MP, 2, BT, HD), BF16),
            pltpu.SemaphoreType.DMA((NBLK,)),
            pltpu.SemaphoreType.DMA((NBLK,)),
            pltpu.SemaphoreType.DMA((2, N_MP)),
            pltpu.SemaphoreType.DMA((2, N_MP)),
            pltpu.SemaphoreType.DMA((4,)),
            pltpu.SemaphoreType.REGULAR,
            pltpu.SemaphoreType.REGULAR,
        ],
        compiler_params=pltpu.CompilerParams(
            collective_id=0, has_side_effects=True, vmem_limit_bytes=56 * 2**20
        ),
        name="prefill_decode",
    )(lengths, row_request, owners, q, k, v, sq, sk, sv)
    results = (out, pk, pv, dec)
    out, pk, pv, dec = pl.pallas_call(
        copy_kernel,
        out_shape=tuple(jax.ShapeDtypeStruct(r.shape, r.dtype) for r in results),
        in_specs=[hbm] * 4,
        out_specs=(hbm,) * 4,
        scratch_shapes=[pltpu.VMEM(r.shape, r.dtype) for r in results]
        + [pltpu.SemaphoreType.DMA((8,))] * 2,
        name="results",
    )(*results)
    shape = (1, 1, 2, BT, N_MP * HD)
    return out, pk.reshape(shape), pv.reshape(shape), dec


def solution(mesh):
    split = P("ctx", "mp")
    steps = P(None, "ctx", "mp")
    paged = P("ctx", "mp", None, None, None)
    return jax.shard_map(
        on_device,
        mesh=mesh,
        in_specs=(split, split, split, steps, steps, steps, P("ctx"), P(), P()),
        out_specs=(split, paged, paged, steps),
        check_vma=False,
    )
```

```python
import functools
import math

import jax
import jax.numpy as jnp
from jax import lax
from jax.experimental import pallas as pl
from jax.experimental.pallas import tpu as pltpu
from jax.sharding import PartitionSpec as P

HEADS = 8
HD = 128
ROWS = 512
HALF = ROWS // 2
BT = 128
NBLK = 16
SEQ = NBLK * ROWS
STEP_ROWS = 128
REACH = 10
NEG = -1e30
C = math.log2(math.e) / math.sqrt(HD)
F32 = jnp.float32
BF16 = jnp.bfloat16
MESH = pl.DeviceIdType.MESH
N_MP = 8


def score(queries, keys):
    return lax.dot_general(queries, keys, (((1,), (1,)), ((), ())), preferred_element_type=F32)


def kernel(
    lengths, row_request, owners,
    q_hbm, k_ref, v_ref, sq_ref, sk_ref, sv_ref,
    out_hbm, dec_ref, pk_ref, pv_ref,
    q_ref, out_ref, kv, mk, mq, acc, tot, high, s0, s1, n0, n1, f0, f1, qd, sd, tail, pages_k, pages_v,
    send_sem, recv_sem, psend_sem, precv_sem, self_sem, ctx_in, mp_in,
):
    ctx = lax.axis_index("ctx")
    mp = lax.axis_index("mp")
    x, y, core = ctx // 4, (ctx // 2) % 2, ctx % 2

    def place(xx, yy, kk):
        return ((xx + 4) % 4) * 4 + yy * 2 + kk

    sib = place(x, y, 1 - core)
    across = place(x, 1 - y, core)
    right = place(x + 1, y, core)
    left = place(x - 1, y, core)

    barrier = pltpu.get_barrier_semaphore()
    for near in (place(x, 1 - y, 0), place(x + 1, y, 0), place(x - 1, y, 0)):
        pl.semaphore_signal(barrier, inc=1, device_id=(near, mp), device_id_type=MESH)
    for d in range(1, N_MP):
        pl.semaphore_signal(
            barrier,
            inc=1,
            device_id=(place(x, y, 1), (mp + d) % N_MP),
            device_id_type=MESH,
        )

    @pl.when(core == 1)
    def _():
        pl.semaphore_signal(barrier, inc=1, device_id=(sib, mp), device_id_type=MESH)

    load_q = pltpu.make_async_copy(q_hbm, q_ref, self_sem.at[2])
    load_q.start()

    def rows_of(block):
        return pl.ds(pl.multiple_of(block * ROWS, ROWS), ROWS)

    own = rows_of(ctx)
    kv[own, :HD] = k_ref[...]
    kv[own, HD:] = v_ref[...]

    def tell(semaphore):
        pl.semaphore_signal(semaphore, inc=1, device_id=(sib, mp), device_id_type=MESH)

    @pl.when(core == 0)
    def _():
        pl.semaphore_wait(barrier, 7)
        tell(ctx_in)

    @pl.when(core == 1)
    def _():
        pl.semaphore_wait(ctx_in, 1)


    def send(block, to, slot):
        return pltpu.make_async_remote_copy(
            src_ref=kv.at[rows_of(block)],
            dst_ref=kv.at[rows_of(block)],
            send_sem=send_sem.at[slot],
            recv_sem=recv_sem.at[block],
            device_id=(to, mp),
            device_id_type=MESH,
        )

    def arrived(block):
        send(block, sib, 0).wait_recv()

    sent = []

    def forward(block, targets):
        for to in targets:
            copy = send(block, to, len(sent))
            copy.start()
            sent.append(copy)

    forward(ctx, (across, right, left, sib))

    lane = lax.broadcasted_iota(jnp.int32, (1, HD), 1)
    e0 = lengths[0]
    e1 = e0 + lengths[1]
    e2 = e1 + lengths[2]
    begin = jnp.where(lane == 1, e0, jnp.where(lane == 2, e1, jnp.where(lane == 3, e2, 0)))
    end = jnp.where(
        lane == 0, e0, jnp.where(lane == 1, e1, jnp.where(lane == 2, e2, jnp.where(lane == 3, SEQ, 0)))
    )

    def belongs(first, count):
        pos = first + lax.broadcasted_iota(jnp.int32, (count, HD), 0)
        return (pos >= begin) & (pos < end)

    def fill(block, _):
        mk[rows_of(block), :] = jnp.where(belongs(block * ROWS, ROWS), 1.0, 0.0).astype(BF16)
        return 0

    lax.fori_loop(0, NBLK, fill, 0)
    wide = lax.broadcasted_iota(jnp.int32, (ROWS, HD), 1)
    mq[...] = jnp.where(belongs(ctx * ROWS, ROWS) | (wide >= 4), 0.0, NEG).astype(BF16)

    own_of = [owners[b] for b in range(4)]
    slot_of = []
    for b in range(4):
        earlier = jnp.int32(0)
        for a in range(b):
            earlier = earlier + jnp.where(own_of[a] == own_of[b], 1, 0)
        slot_of.append(earlier)

    def fill_page(t, _):
        o, s = t // 2, t % 2
        picked_k = jnp.zeros((BT, HD), F32)
        picked_v = jnp.zeros((BT, HD), F32)
        for b in range(4):
            hit = jnp.where((own_of[b] == o) & (slot_of[b] == s), 1.0, 0.0).astype(F32)
            picked_k = picked_k + hit * k_ref[b * BT : (b + 1) * BT, :].astype(F32)
            picked_v = picked_v + hit * v_ref[b * BT : (b + 1) * BT, :].astype(F32)
        pages_k[o, s] = picked_k.astype(BF16)
        pages_v[o, s] = picked_v.astype(BF16)
        return 0

    lax.fori_loop(0, 2 * N_MP, fill_page, 0)
    mine = pl.ds(pl.multiple_of(mp * HD, HD), HD)
    pages = ((pages_k, pk_ref), (pages_v, pv_ref))

    def page_copies():
        copies = []
        for d in range(1, N_MP):
            to = (mp + d) % N_MP
            for i, (source, target) in enumerate(pages):
                copies.append(
                    pltpu.make_async_remote_copy(
                        src_ref=source.at[to],
                        dst_ref=target.at[:, :, mine],
                        send_sem=psend_sem.at[i, d],
                        recv_sem=precv_sem.at[i, d],
                        device_id=(ctx, to),
                        device_id_type=MESH,
                    )
                )
        return copies

    def send_pages():
        @pl.when(core == 1)
        def _():
            pl.semaphore_wait(barrier, 2 * (N_MP - 1))
            tell(mp_in)

        @pl.when(core == 0)
        def _():
            pl.semaphore_wait(mp_in, 1)

        for copy in page_copies():
            copy.start()

    kept = []
    for i, (source, target) in enumerate(pages):
        copy = pltpu.make_async_copy(source.at[mp], target.at[:, :, mine], self_sem.at[i])
        copy.start()
        kept.append(copy)

    def tile_of(h, first=0, count=ROWS):
        return pl.ds(pl.multiple_of(h * ROWS + first, HALF), count)

    def bands(diagonal):
        return ((0, HALF, HALF), (HALF, HALF, ROWS)) if diagonal else ((0, ROWS, ROWS),)

    def produce(h, blocks, s_ref, n_ref, f_ref, diagonal, fresh):
        for first, count, columns in bands(diagonal):
            rows = pl.ds(first, count)
            queries = jnp.concatenate(
                [q_ref[rows, pl.ds(pl.multiple_of(h * HD, HD), HD)], mq[rows, :]], axis=1
            )
            best = None
            for i, block in enumerate(blocks):
                span = pl.ds(pl.multiple_of(block * ROWS, ROWS), columns)
                s = score(queries, jnp.concatenate([kv[span, :HD], mk[span, :]], axis=1))
                if diagonal:
                    at = lax.broadcasted_iota(jnp.int32, s.shape, 0) + first
                    s = jnp.where(at >= lax.broadcasted_iota(jnp.int32, s.shape, 1), s, NEG)
                s_ref[rows, i * columns : (i + 1) * columns] = s
                for j in range(0, columns, HD):
                    part = s[:, j : j + HD]
                    best = part if best is None else jnp.maximum(best, part)
            best = jnp.max(best, axis=1, keepdims=True)
            if fresh:
                n_ref[rows, :] = jnp.broadcast_to(best, (count, HD))
            else:
                before = high[tile_of(h, first, count), :]
                now = jnp.maximum(before, best)
                n_ref[rows, :] = now
                f_ref[rows, :] = jnp.exp2((before - now) * C)

    def consume(h, blocks, s_ref, n_ref, f_ref, diagonal, fresh):
        for first, count, columns in bands(diagonal):
            rows = pl.ds(first, count)
            at = tile_of(h, first, count)
            now = n_ref[rows, :]
            total = None
            running = None
            for i, block in enumerate(blocks):
                span = pl.ds(pl.multiple_of(block * ROWS, ROWS), columns)
                parts = []
                for j in range(i * columns, (i + 1) * columns, HD):
                    weight = jnp.exp2((s_ref[rows, j : j + HD] - now) * C)
                    total = weight if total is None else total + weight
                    parts.append(weight.astype(BF16))
                product = jnp.dot(
                    jnp.concatenate(parts, axis=1), kv[span, HD:], preferred_element_type=F32
                )
                running = product if running is None else running + product
            high[at, :] = now
            if fresh:
                acc[at, :] = running
                tot[at, :] = total
            else:
                fade = f_ref[rows, :]
                acc[at, :] = acc[at, :] * fade + running
                tot[at, :] = tot[at, :] * fade + total

    def stage(work, h, odd, blocks, diagonal=False, fresh=False):
        slot = (s1, n1, f1) if odd else (s0, n0, f0)
        work(h, blocks, *slot, diagonal, fresh)

    def attend(blocks, diagonal=False, fresh=False):
        kind = (blocks, diagonal, fresh)
        stage(produce, 0, 0, *kind)

        def body(i, _):
            stage(produce, 2 * i + 1, 1, *kind)
            stage(consume, 2 * i, 0, *kind)
            stage(produce, 2 * i + 2, 0, *kind)
            stage(consume, 2 * i + 1, 1, *kind)
            return 0

        lax.fori_loop(0, HEADS // 2 - 1, body, 0)
        stage(produce, HEADS - 1, 1, *kind)
        stage(consume, HEADS - 2, 0, *kind)
        stage(consume, HEADS - 1, 1, *kind)

    load_q.wait()
    attend((ctx,), diagonal=True, fresh=True)

    chip = ctx // 2

    def nth(n):
        rank = (n - core + 2) // 2 - 1
        near = rank + 1
        swapped = jnp.minimum(rank + 2 - 2 * ((rank + 2) % 2), 5)
        before = jnp.where(y == 1, near, swapped)
        inside = 1 - (n - core + 2) % 2
        return jnp.where((n == 0) & (core == 1), sib, (chip - before) * 2 + inside)

    count = jnp.minimum(ctx, REACH)

    def spot(dx, dy, other_core):
        return place(x + dx, (y + dy) % 2, (core + other_core) % 2)

    def event(dx, dy, targets):
        block = spot(dx, dy, 0)
        arrived(block)
        forward(block, targets + (sib,))

    def mirrored(dx, dy):
        arrived(spot(dx, dy, 1))

    def events(step):
        if step == 0:
            mirrored(0, 0)
            event(0, 1, (right, left))
            event(-1, 0, (right,))

            @pl.when(y == 1)
            def _():
                mirrored(0, 1)

            @pl.when(y == 0)
            def _():
                mirrored(-1, 0)

        if step == 1:
            event(1, 0, ())
            event(1, 1, (left,))
            event(-1, 1, ())

            @pl.when(y == 1)
            def _():
                mirrored(-1, 0)

            @pl.when(y == 0)
            def _():
                mirrored(0, 1)
                mirrored(-1, 1)

        if step == 2:
            mirrored(1, 0)
            mirrored(1, 1)

            @pl.when(y == 1)
            def _():
                mirrored(-1, 1)

            event(2, 0, ())
            mirrored(2, 0)
        if step == 3:
            event(2, 1, ())
            mirrored(2, 1)

    many = count >= REACH - 1
    pairs = jnp.where(many, (count - 6) // 2, REACH // 2)

    def one_step(step, _):
        for at in range(3):

            @pl.when(step == at)
            def _(at=at):
                events(at)
                if at == 0:
                    send_pages()
                if at == 2:
                    events(3)

        @pl.when((2 * step + 1 < count) & (step < pairs))
        def _():
            attend((nth(2 * step), nth(2 * step + 1)))

        @pl.when((count % 2 == 1) & (step == jnp.where(many, 1, 4)))
        def _():
            attend((nth(jnp.where(many, 2, count - 1)),))

        return 0

    lax.fori_loop(0, REACH // 2, one_step, 0)

    @pl.when(many)
    def _():
        attend(tuple(nth(count - 6 + n) for n in range(6)))

    def finished(h):
        at = pl.ds(pl.multiple_of(h * ROWS, ROWS), ROWS)
        total = jnp.sum(tot[at, :], axis=1, keepdims=True)
        return (acc[at, :] / total).astype(BF16)

    def finish(h, _):
        out_ref[:, pl.ds(pl.multiple_of(h * HD, HD), HD)] = finished(h)
        return 0

    lax.fori_loop(0, HEADS, finish, 0)
    store_out = pltpu.make_async_copy(out_ref, out_hbm, self_sem.at[3])
    store_out.start()

    for h in range(HEADS):
        for t in range(2):
            qd[h * 4 + t * 2 : h * 4 + t * 2 + 2, :HD] = sq_ref[
                t, :, h * HD : (h + 1) * HD
            ].astype(F32)
    drow = lax.broadcasted_iota(jnp.int32, (4 * HEADS, HD), 0)
    dlane = lax.broadcasted_iota(jnp.int32, (4 * HEADS, HD), 1)
    drow_t, drow_r = (drow & 3) >> 1, drow & 1
    asked = jnp.where(drow_r == 0, row_request[ctx * 2], row_request[ctx * 2 + 1])
    key_u, key_r = ((dlane - 4) & 3) >> 1, (dlane - 4) & 1
    allowed = ((dlane < 4) & (dlane == asked)) | (
        (dlane >= 4) & (dlane < 8) & (key_r == drow_r) & (key_u <= drow_t)
    )
    qd[:, HD:] = jnp.where(allowed | (dlane > 8), 0.0, NEG)
    queries = qd[...].astype(BF16)
    tail[...] = jnp.zeros_like(tail)
    for t in range(2):
        tail[t * 2 : t * 2 + 2, :HD] = sk_ref[t].astype(F32)
        tail[t * 2 : t * 2 + 2, HD:] = sv_ref[t].astype(F32)
    trow = lax.broadcasted_iota(jnp.int32, (STEP_ROWS, HD), 0)
    tlane = lax.broadcasted_iota(jnp.int32, (STEP_ROWS, HD), 1)
    tmask = jnp.where(tlane == jnp.where(trow < 4, trow + 4, 8), 1.0, 0.0).astype(BF16)
    s = score(queries, jnp.concatenate([tail[:, :HD].astype(BF16), tmask], axis=1))
    sd[:, SEQ:] = s
    best = s
    chunk = 1024
    for k in range(0, SEQ, chunk):
        s = score(queries, jnp.concatenate([kv[k : k + chunk, :HD], mk[k : k + chunk, :]], axis=1))
        sd[:, k : k + chunk] = s
        for j in range(0, chunk, HD):
            best = jnp.maximum(best, s[:, j : j + HD])
    best = jnp.max(best, axis=1, keepdims=True)
    weight = jnp.exp2((sd[:, SEQ:] - best) * C)
    total = weight
    running = jnp.dot(weight.astype(BF16), tail[:, HD:].astype(BF16), preferred_element_type=F32)
    for k in range(0, SEQ, chunk):
        parts = []
        for j in range(k, k + chunk, HD):
            weight = jnp.exp2((sd[:, j : j + HD] - best) * C)
            total = total + weight
            parts.append(weight.astype(BF16))
        running = running + jnp.dot(
            jnp.concatenate(parts, axis=1), kv[k : k + chunk, HD:], preferred_element_type=F32
        )
    result = running / jnp.sum(total, axis=1, keepdims=True)
    for h in range(HEADS):
        for t in range(2):
            dec_ref[t, :, h * HD : (h + 1) * HD] = result[
                h * 4 + t * 2 : h * 4 + t * 2 + 2, :
            ].astype(BF16)

    for slot in range(len(sent)):
        send(ctx, sib, slot).wait_send()
    for copy in kept:
        copy.wait()
    for copy in page_copies():
        copy.wait()
    store_out.wait()


def copy_kernel(out, pk, pv, dec, out_to, pk_to, pv_to, dec_to, *scratch):
    held, (sem_in, sem_out) = scratch[:-2], scratch[-2:]
    parts = []
    for a, via, b, count in zip(
        (out, pk, pv, dec), held, (out_to, pk_to, pv_to, dec_to), (4, 2, 2, 2)
    ):
        for i in range(count):
            size = a.shape[0] // count
            span = pl.ds(i * size, size)
            n = len(parts)
            parts.append(
                (
                    pltpu.make_async_copy(a.at[span], via.at[span], sem_in.at[n]),
                    pltpu.make_async_copy(via.at[span], b.at[span], sem_out.at[n]),
                )
            )
    for inward, _ in parts:
        inward.start()
    for inward, outward in parts:
        inward.wait()
        outward.start()
    for _, outward in parts:
        outward.wait()


def on_device(q, k, v, sq, sk, sv, owners, lengths, row_request):
    vmem = pl.BlockSpec(memory_space=pltpu.VMEM)
    smem = pl.BlockSpec(memory_space=pltpu.SMEM)
    hbm = pl.BlockSpec(memory_space=pl.ANY)
    out, dec, pk, pv = pl.pallas_call(
        kernel,
        out_shape=(
            jax.ShapeDtypeStruct((ROWS, HEADS * HD), BF16),
            jax.ShapeDtypeStruct(sq.shape, BF16),
            jax.ShapeDtypeStruct((2, BT, N_MP * HD), BF16),
            jax.ShapeDtypeStruct((2, BT, N_MP * HD), BF16),
        ),
        in_specs=[smem] * 3 + [hbm] + [vmem] * 5,
        out_specs=(hbm, vmem, hbm, hbm),
        scratch_shapes=[
            pltpu.VMEM((ROWS, HEADS * HD), BF16),
            pltpu.VMEM((ROWS, HEADS * HD), BF16),
            pltpu.VMEM((SEQ, 2 * HD), BF16),
            pltpu.VMEM((SEQ, HD), BF16),
            pltpu.VMEM((ROWS, HD), BF16),
            pltpu.VMEM((HEADS * ROWS, HD), F32),
            pltpu.VMEM((HEADS * ROWS, HD), F32),
            pltpu.VMEM((HEADS * ROWS, HD), F32),
            pltpu.VMEM((ROWS, 6 * ROWS), F32),
            pltpu.VMEM((ROWS, 6 * ROWS), F32),
            pltpu.VMEM((ROWS, HD), F32),
            pltpu.VMEM((ROWS, HD), F32),
            pltpu.VMEM((ROWS, HD), F32),
            pltpu.VMEM((ROWS, HD), F32),
            pltpu.VMEM((4 * HEADS, 2 * HD), F32),
            pltpu.VMEM((4 * HEADS, SEQ + STEP_ROWS), F32),
            pltpu.VMEM((STEP_ROWS, 2 * HD), F32),
            pltpu.VMEM((N_MP, 2, BT, HD), BF16),
            pltpu.VMEM((N_MP, 2, BT, HD), BF16),
            pltpu.SemaphoreType.DMA((NBLK,)),
            pltpu.SemaphoreType.DMA((NBLK,)),
            pltpu.SemaphoreType.DMA((2, N_MP)),
            pltpu.SemaphoreType.DMA((2, N_MP)),
            pltpu.SemaphoreType.DMA((4,)),
            pltpu.SemaphoreType.REGULAR,
            pltpu.SemaphoreType.REGULAR,
        ],
        compiler_params=pltpu.CompilerParams(
            collective_id=0, has_side_effects=True, vmem_limit_bytes=56 * 2**20
        ),
        name="prefill_decode",
    )(lengths, row_request, owners, q, k, v, sq, sk, sv)
    results = (out, pk, pv, dec)
    out, pk, pv, dec = pl.pallas_call(
        copy_kernel,
        out_shape=tuple(jax.ShapeDtypeStruct(r.shape, r.dtype) for r in results),
        in_specs=[hbm] * 4,
        out_specs=(hbm,) * 4,
        scratch_shapes=[pltpu.VMEM(r.shape, r.dtype) for r in results]
        + [pltpu.SemaphoreType.DMA((10,))] * 2,
        name="results",
    )(*results)
    shape = (1, 1, 2, BT, N_MP * HD)
    return out, pk.reshape(shape), pv.reshape(shape), dec


def solution(mesh):
    split = P("ctx", "mp")
    steps = P(None, "ctx", "mp")
    paged = P("ctx", "mp", None, None, None)
    return jax.shard_map(
        on_device,
        mesh=mesh,
        in_specs=(split, split, split, steps, steps, steps, P("ctx"), P(), P()),
        out_specs=(split, paged, paged, steps),
        check_vma=False,
    )
```
